512 devices in a mesh: pi: 16 (over x, z_hi, core), pj: 32 (over z_lo, y).
Axes of the slice: x: 4, y: 4, z: 16 (z_hi: 2, z_lo: 8; z = z_hi * 8 + z_lo), core: 2. Of those that a mesh axis runs over, the one named last changes fastest.
Arguments:
- amplitudes: bfloat16 [32, 32, 128, 128], P('pi', 'pj'), may hold values from -6 to 6
- cholesky: bfloat16 [128, 128, 4096], P(None, None, 'pj'), may hold values from -1 to 1, as said below
- other_terms: float32 [32, 32, 128, 128], P('pi', 'pj'), may hold values from -6 to 6
Outputs:
- residual: float32 [32, 32, 128, 128], P('pi', 'pj')
The draws below stay inside these ranges and needn't reach their ends.
Inputs may be any that keep to these rules, and one draw needn't show every extreme that they name: cholesky[x, y, P] equals cholesky[y, x, P].
All inputs are finite; a program needn't handle non-finite values.
Results may differ from the reference program's by a relative error of at most 0.0036.
Values may be sent and summed in bfloat16 or wider, within the bound.
A program may use at most 64 MiB of HBM per device.

```python
import math
import jax
import jax.numpy as jnp
from jax import lax

NV = 128
NCHOL = 4096
NOCC = 32


def draw_cholesky(key, part):
    scale = 1.0 / math.sqrt(NV * math.sqrt(NCHOL))
    base = jax.random.truncated_normal(key, -6.0, 6.0, (NV, NV, NCHOL), jnp.float32)
    sym = (base + jnp.swapaxes(base, 0, 1)) * (scale / math.sqrt(2.0))
    return sym.astype(jnp.bfloat16)


def shard_levels(stream_key, extent, pieces, smallest, largest):
    def one(axis_at, parts):
        heights = jax.random.uniform(jax.random.fold_in(jax.random.fold_in(stream_key, 6), axis_at), (parts,), jnp.float32, smallest / len(pieces), largest / len(pieces))
        return jnp.repeat(jnp.exp(heights), extent[axis_at] // parts).reshape((-1,) + (1,) * (len(extent) - axis_at - 1))

    level = one(*pieces[0])
    for cut in pieces[1:]:
        level = level * one(*cut)
    return level


def scatter_about(rng, shape, spread, limit, pieces=(), kind=jnp.bfloat16):
    entries = spread * jax.random.normal(rng, shape, jnp.float32)
    if pieces:
        entries = entries * shard_levels(rng, shape, pieces, -0.22, 0.18)
    return jnp.clip(entries, -limit, limit).astype(kind)


def setup_inputs(seed: int = 0) -> dict:
    arg_keys = jax.random.split(jax.random.key(seed), 4)
    return {
        "amplitudes": scatter_about(arg_keys[0], (NOCC, NOCC, NV, NV), 1.0, 6.0, ((0, 16), (1, 32))),
        "cholesky": draw_cholesky(jax.random.fold_in(arg_keys[3], 71), 0),
        "other_terms": scatter_about(arg_keys[2], (NOCC, NOCC, NV, NV), 1.0, 6.0, ((0, 16), (1, 32)), jnp.float32),
    }


def reference(amplitudes, cholesky, other_terms):
    vectors = cholesky.astype(jnp.float32)
    pairs = amplitudes.astype(jnp.float32)

    def one_virtual(index):
        left = lax.dynamic_index_in_dim(vectors, index, 0, keepdims=False)
        tile = jnp.einsum("cp,bdp->bcd", left, vectors).astype(jnp.bfloat16)
        tile = lax.optimization_barrier(tile).astype(jnp.float32)
        return jnp.einsum("ijcd,bcd->ijb", pairs, tile)

    stacked = lax.map(one_virtual, jnp.arange(NV, dtype=jnp.int32))
    ladder = jnp.transpose(stacked, (1, 2, 0, 3))
    half = (other_terms + 0.5 * ladder).astype(jnp.bfloat16)
    wide = lax.optimization_barrier(half).astype(jnp.float32)
    return wide + jnp.transpose(wide, (1, 0, 3, 2))
```

```python
import jax
import jax.numpy as jnp
from jax import lax
from jax.sharding import PartitionSpec as P


def spread(block, axis):
    count = lax.axis_size(axis)
    copies = jnp.broadcast_to(block[None], (count,) + block.shape)
    return lax.all_to_all(copies, axis, split_axis=0, concat_axis=0, tiled=True)


def mirror_route(count_i, count_j, turn):
    route = []
    for row in range(count_i):
        for col in range(count_j):
            target = (col // 2) * count_j + 2 * row + (turn + col) % 2
            route.append((row * count_j + col, target))
    return route


def shards(amplitudes, cholesky, other_terms):
    width = cholesky.shape[0]
    pair_i = amplitudes.shape[0]
    count_i = lax.axis_size("pi")
    count_j = lax.axis_size("pj")
    depth = cholesky.shape[2]
    block_i = width // count_i
    block_j = width // count_j
    row_index = lax.axis_index("pi")
    col_index = lax.axis_index("pj")
    split = lax.all_to_all(
        amplitudes[:, 0], "pi", split_axis=1, concat_axis=0, tiled=True
    )
    gathered = spread(split, "pj")
    own_rows = lax.dynamic_slice_in_dim(cholesky, row_index * block_i, block_i, 0)
    from_i = spread(own_rows, "pj")
    from_j = lax.all_to_all(
        cholesky.reshape(count_j, block_j, width, depth), "pj", 0, 0, tiled=True
    )
    total = jnp.einsum("kcap,kbdp->cdba", from_i, from_j, preferred_element_type=jnp.float32)
    tile = total.astype(jnp.bfloat16)
    sums = jnp.einsum("jicd,cdba->ijba", gathered, tile, preferred_element_type=jnp.float32)
    parts = lax.all_to_all(
        sums.reshape(count_i, pair_i, count_j, block_j, width), "pi", 0, 0, tiled=True
    )
    summed = jnp.sum(parts, axis=0)
    ladder = lax.all_to_all(summed, "pj", split_axis=1, concat_axis=1, tiled=True)
    ladder = ladder.reshape(pair_i, width, width).swapaxes(1, 2)
    half = (other_terms[:, 0] + 0.5 * ladder).astype(jnp.bfloat16)
    odd = col_index % 2 == 1
    received = []
    for turn in range(2):
        outgoing = jnp.where(odd, half[1 - turn], half[turn])
        received.append(
            lax.ppermute(outgoing, ("pi", "pj"), mirror_route(count_i, count_j, turn))
        )
    first = jnp.where(odd, received[1], received[0])
    second = jnp.where(odd, received[0], received[1])
    mirrored = jnp.stack([first, second]).swapaxes(1, 2)
    return (half.astype(jnp.float32) + mirrored.astype(jnp.float32))[:, None]


def solution(mesh):
    return jax.shard_map(
        shards,
        mesh=mesh,
        in_specs=(P("pi", "pj", None, None), P(None, None, "pj"), P("pi", "pj", None, None)),
        out_specs=P("pi", "pj", None, None),
        check_vma=False,
    )
```

```python
import jax
import jax.numpy as jnp
from jax import lax
from jax.experimental import pallas as pl
from jax.experimental.pallas import tpu as pltpu
from jax.sharding import PartitionSpec as P

MESH = pl.DeviceIdType.MESH
NY = 4
NZ = 8
STEP = 8
F32 = jnp.float32
BF16 = jnp.bfloat16


def kept_of(row, col):
    return (col % 2) if row <= col // 2 else 1 - col % 2


def routes(count_i, count_j):
    there, back = [], []
    for row in range(count_i):
        for col in range(count_j):
            kept = kept_of(row, col)
            other = 1 - kept
            side = col // 2
            me = row * count_j + col
            there.append((me, side * count_j + 2 * row + other))
            pick = other if side == row else kept
            back.append((me, side * count_j + 2 * row + pick))
    return there, back


def ladder_kernel(
    vec, own, out,
    pairs, extra, work, acc, acc_own, acc_x, part, part_x, got_y, got_yx, got_z, got_zx, send_z, send_zx,
    zs, zr, ys, yr, xs, xr, rs, rr, rxs, rxr, ss, sr, sxs, sxr,
):
    row = lax.axis_index("pi")
    col = lax.axis_index("pj")
    y = lax.rem(col, NY)
    z = col // NY
    n = vec.shape[1]
    count = NY * NZ
    col_x = 2 * row + 1
    y_x = lax.rem(col_x, NY)
    z_x = col_x // NY

    def at(zz, yy):
        return (row, zz * NY + yy)

    def copy(src, dst, s, r, to):
        return pltpu.make_async_remote_copy(src, dst, s, r, device_id=to, device_id_type=MESH)

    barrier = pltpu.get_barrier_semaphore()

    def greet(k, _):
        pl.semaphore_signal(
            barrier, 1, device_id=(row, lax.rem(col + k, count)), device_id_type=MESH
        )
        return 0

    lax.fori_loop(1, count, greet, 0)
    pl.semaphore_wait(barrier, count - 1)

    def z_copy(k):
        to = lax.rem(z + k, NZ)
        return copy(own.at[0], pairs.at[y, z], zs.at[k], zr.at[k], at(to, y))

    for k in range(1, NZ):
        z_copy(k).start()

    def x_copy(k):
        return copy(own.at[1], extra, xs.at[k], xr, (row, lax.rem(col + k, count)))

    is_x = col == col_x

    @pl.when(is_x)
    def _():
        def go(k, _):
            x_copy(k).start()
            return 0

        lax.fori_loop(1, count, go, 0)

    pairs[y, z] = own[0]
    for k in range(1, NZ):
        copy(
            own.at[0], pairs.at[y, lax.rem(z + NZ - k, NZ)], zs.at[k], zr.at[k], at(z, y)
        ).wait_recv()

    def y_copy(k):
        return copy(pairs.at[y], pairs.at[y], ys.at[k], yr.at[k], at(z, lax.rem(y + k, NY)))

    for k in range(1, NY):
        y_copy(k).start()

    def first(block, index, slot, wide):
        lp = vec[pl.ds(pl.multiple_of(index * STEP * n, STEP * n), STEP * n), :]
        work[slot, :, 0 : wide * n] = jnp.dot(
            lp, block, preferred_element_type=F32
        ).astype(BF16)

    def second(index, slot, wide):
        lp = vec[pl.ds(pl.multiple_of(index * STEP * n, STEP * n), STEP * n), :]
        rows = []
        for p in range(wide):
            tiles = [
                work[slot, q * n : (q + 1) * n, p * n : (p + 1) * n] for q in range(STEP)
            ]
            rows.append(jnp.concatenate(tiles, axis=1))
        lhs = jnp.concatenate(rows, axis=0)
        acc[0 : wide * n, :] += jnp.dot(lhs, lp, preferred_element_type=F32)

    def group(yg, with_extra):
        wide = NZ + 1 if with_extra else NZ
        steps = n // STEP

        def block():
            tiles = [pairs[yg, k] for k in range(NZ)]
            if with_extra:
                tiles.append(extra[...])
            return jnp.concatenate(tiles, axis=1)

        acc[...] = jnp.zeros_like(acc)
        first(block(), 0, 0, wide)

        def step(index, _):
            slot = lax.rem(index, 2)
            first(block(), jnp.minimum(index + 1, steps - 1), 1 - slot, wide)
            second(index, slot, wide)
            return 0

        lax.fori_loop(0, steps, step, 0)

    def r_copy(k):
        return copy(
            part.at[k], got_y.at[k], rs.at[k], rr.at[k], at(z, lax.rem(y + NY - k, NY))
        )

    def y_wait(k):
        source = lax.rem(y + NY - k, NY)
        copy(pairs.at[y], pairs.at[source], ys.at[k], yr.at[k], at(z, y)).wait_recv()

    group(y, False)
    acc_own[...] = acc[0 : NZ * n, :]

    def turn(k, _):
        y_wait(k)
        group(lax.rem(y + NY - k, NY), False)
        part[k] = acc[0 : NZ * n, :].astype(BF16).reshape(NZ, n, n)
        r_copy(k).start()
        return 0

    lax.fori_loop(1, NY - 1, turn, 0)

    last = NY - 1
    y_wait(last)

    @pl.when(is_x)
    def _():
        extra[...] = own[1]

    @pl.when(jnp.logical_not(is_x))
    def _():
        x_copy(0).wait_recv()

    group(lax.rem(y + 1, NY), True)
    part[last] = acc[0 : NZ * n, :].astype(BF16).reshape(NZ, n, n)
    r_copy(last).start()
    part_x[...] = acc[NZ * n :, :].astype(BF16)
    acc_x[...] = acc[NZ * n :, :]

    on_y = y == y_x
    gap_y = lax.rem(y_x + NY - y, NY)

    def rx_copy(k):
        return copy(part_x, got_yx.at[k], rxs, rxr.at[k], at(z, y_x))

    @pl.when(jnp.logical_not(on_y))
    def _():
        rx_copy(gap_y).start()

    for k in range(1, NY):
        copy(part.at[k], got_y.at[k], rs.at[k], rr.at[k], at(z, y)).wait_recv()
    send_z[...] = (
        acc_own[...].reshape(NZ, n, n)
        + got_y[1].astype(F32) + got_y[2].astype(F32) + got_y[3].astype(F32)
    ).astype(BF16)

    def s_copy(k):
        to = lax.rem(z + k, NZ)
        return copy(send_z.at[to], got_z.at[k], ss.at[k], sr.at[k], at(to, y))

    for k in range(1, NZ):
        s_copy(k).start()

    on_x = jnp.logical_and(on_y, z == z_x)
    near_x = jnp.logical_and(on_y, z != z_x)
    gap_z = lax.rem(z_x + NZ - z, NZ)

    def sx_copy(k):
        return copy(send_zx, got_zx.at[k], sxs, sxr.at[k], at(z_x, y))

    @pl.when(on_y)
    def _():
        for k in range(1, NY):
            copy(part_x, got_yx.at[k], rxs, rxr.at[k], at(z, y)).wait_recv()
        acc_x[...] += (
            got_yx[1].astype(F32) + got_yx[2].astype(F32) + got_yx[3].astype(F32)
        )
        send_zx[...] = acc_x[...].astype(BF16)

    @pl.when(near_x)
    def _():
        sx_copy(gap_z).start()

    total = send_z[z].astype(F32)
    for k in range(1, NZ):
        copy(send_z.at[z], got_z.at[k], ss.at[k], sr.at[k], at(z, y)).wait_recv()
        total = total + got_z[k].astype(F32)
    out[0] = total
    out[1] = acc_x[...]

    @pl.when(on_x)
    def _():
        whole = acc_x[...]
        for k in range(1, NZ):
            copy(send_zx, got_zx.at[k], sxs, sxr.at[k], at(z, y)).wait_recv()
            whole = whole + got_zx[k].astype(F32)
        out[1] = whole

    for k in range(1, NZ):
        z_copy(k).wait_send()
        s_copy(k).wait_send()
    for k in range(1, NY):
        y_copy(k).wait_send()
        r_copy(k).wait_send()

    @pl.when(is_x)
    def _():
        def end(k, _):
            x_copy(k).wait_send()
            return 0

        lax.fori_loop(1, count, end, 0)

    @pl.when(jnp.logical_not(on_y))
    def _():
        rx_copy(gap_y).wait_send()

    @pl.when(near_x)
    def _():
        sx_copy(gap_z).wait_send()


def ladder_of(vectors, own):
    n = own.shape[-1]
    dma = pltpu.SemaphoreType.DMA
    vmem = pltpu.VMEM
    return pl.pallas_call(
        ladder_kernel,
        out_shape=jax.ShapeDtypeStruct((2, n, n), F32),
        in_specs=[pl.BlockSpec(memory_space=vmem)] * 2,
        out_specs=pl.BlockSpec(memory_space=vmem),
        scratch_shapes=[
            vmem((NY, NZ, n, n), BF16),
            vmem((n, n), BF16),
            vmem((2, STEP * n, (NZ + 1) * n), BF16),
            vmem(((NZ + 1) * n, n), F32),
            vmem((NZ * n, n), F32),
            vmem((n, n), F32),
            vmem((NY, NZ, n, n), BF16),
            vmem((n, n), BF16),
            vmem((NY, NZ, n, n), BF16),
            vmem((NY, n, n), BF16),
            vmem((NZ, n, n), BF16),
            vmem((NZ, n, n), BF16),
            vmem((NZ, n, n), BF16),
            vmem((n, n), BF16),
            dma((NZ,)), dma((NZ,)),
            dma((NY,)), dma((NY,)),
            dma((NY * NZ,)), dma,
            dma((NY,)), dma((NY,)),
            dma, dma((NY,)),
            dma((NZ,)), dma((NZ,)),
            dma, dma((NZ,)),
        ],
        compiler_params=pltpu.CompilerParams(
            collective_id=0, has_side_effects=True, vmem_limit_bytes=56 * 2**20
        ),
    )(vectors, own)


def shards(amplitudes, cholesky, other_terms):
    n = cholesky.shape[0]
    count_i = lax.axis_size("pi")
    count_j = lax.axis_size("pj")
    row = lax.axis_index("pi")
    col = lax.axis_index("pj")
    there, back = routes(count_i, count_j)
    side = col // 2
    diagonal = row == side
    second = jnp.where(row <= side, col % 2 == 1, col % 2 == 0)

    def pick(pair, which):
        return jnp.where(which, pair[1], pair[0])

    a = amplitudes[:, 0]
    o = other_terms[:, 0]
    a_kept, a_other = pick(a, second), pick(a, ~second)
    o_kept, o_other = pick(o, second), pick(o, ~second)
    axes = ("pi", "pj")
    a_in = lax.ppermute(a_other, axes, there)
    o_in = lax.ppermute(o_other, axes, there)
    mate = jnp.where(diagonal, a_kept, a_in).astype(F32)
    kept = a_kept.astype(F32) + mate.T
    extra = a_other.astype(F32) + a_in.astype(F32).T
    own = jnp.stack([kept, extra]).astype(BF16)
    vectors = jnp.transpose(cholesky, (2, 0, 1)).reshape(-1, n)
    ladder = ladder_of(vectors, own)
    o_mate = jnp.where(diagonal, o_kept, o_in)
    res_kept = o_kept + o_mate.T + 0.5 * ladder[0]
    res_extra = o_other + o_in.T + 0.5 * ladder[1]
    outgoing = jnp.where(diagonal, res_extra, res_kept)
    incoming = lax.ppermute(outgoing, axes, back).T
    keep_extra = jnp.logical_and(diagonal, col % 2 == 1)
    res_other = jnp.where(keep_extra, res_extra, incoming)
    low = jnp.where(second, res_other, res_kept)
    high = jnp.where(second, res_kept, res_other)
    return jnp.stack([low, high])[:, None]


def solution(mesh):
    return jax.shard_map(
        shards,
        mesh=mesh,
        in_specs=(P("pi", "pj", None, None), P(None, None, "pj"), P("pi", "pj", None, None)),
        out_specs=P("pi", "pj", None, None),
        check_vma=False,
    )
```

```python
import jax
import jax.numpy as jnp
from jax import lax
from jax.experimental import pallas as pl
from jax.experimental.pallas import tpu as pltpu
from jax.sharding import PartitionSpec as P

MESH = pl.DeviceIdType.MESH
NY = 4
NZ = 8
STEP = 16
F32 = jnp.float32
BF16 = jnp.bfloat16


def kept_of(row, col):
    return (col % 2) if row <= col // 2 else 1 - col % 2


def routes(count_i, count_j):
    there, back = [], []
    for row in range(count_i):
        for col in range(count_j):
            kept = kept_of(row, col)
            other = 1 - kept
            side = col // 2
            me = row * count_j + col
            there.append((me, side * count_j + 2 * row + other))
            pick = other if side == row else kept
            back.append((me, side * count_j + 2 * row + pick))
    return there, back


def ladder_kernel(
    vec, own, out,
    pairs, extra, work, acc, acc_own, acc_x, part, part_x, got_z, got_zx, total, send_y, got_y, send_yx, got_yx,
    hs, hr, zs, zr, fs, fr, xs, xr, rs, rr, rxs, rxr, ss, sr, sxs, sxr,
):
    row = lax.axis_index("pi")
    col = lax.axis_index("pj")
    y = lax.rem(col, NY)
    z = col // NY
    n = vec.shape[1]
    count = NY * NZ
    steps = n // STEP
    col_x = 2 * row + 1
    y_x = lax.rem(col_x, NY)
    z_x = col_x // NY

    def at(zz, yy):
        return (row, zz * NY + yy)

    def bits(v):
        return (v % 2, (v // 2) % 2, v // 4)

    def across(v):
        return sum(((a + b) % 2) * 2**k for k, (a, b) in enumerate(zip(bits(z), bits(v))))

    def ahead(k):
        return lax.rem(y + k, NY)

    def copy(src, dst, s, r, to):
        return pltpu.make_async_remote_copy(src, dst, s, r, device_id=to, device_id_type=MESH)

    barrier = pltpu.get_barrier_semaphore()

    def greet(k, _):
        pl.semaphore_signal(
            barrier, 1, device_id=(row, lax.rem(col + k, count)), device_id_type=MESH
        )
        return 0

    lax.fori_loop(1, count, greet, 0)
    pl.semaphore_wait(barrier, count - 1)

    def h_copy(k):
        return copy(own.at[0], pairs.at[0, y], hs.at[k], hr.at[k], at(z, ahead(k)))

    def z_copy(k):
        return copy(own.at[0], pairs.at[k, y], zs.at[k], zr.at[k], at(across(k), y))

    def f_copy(k, j):
        m = k * NY + j
        return copy(pairs.at[k, y], pairs.at[k, y], fs.at[m], fr.at[m], at(z, ahead(j)))

    def x_copy(k):
        return copy(own.at[1], extra, xs.at[k], xr, (row, lax.rem(col + k, count)))

    def r_copy(k):
        return copy(part.at[k], got_z.at[k], rs.at[k], rr.at[k], at(across(k), y))

    def s_copy(k):
        return copy(send_y.at[ahead(k)], got_y.at[k], ss.at[k], sr.at[k], at(z, ahead(k)))

    for k in range(1, NY):
        h_copy(k).start()
    for k in range(1, NZ):
        z_copy(k).start()
    is_x = col == col_x

    @pl.when(is_x)
    def _():
        def go(k, _):
            x_copy(k).start()
            return 0

        lax.fori_loop(1, count, go, 0)
        extra[...] = own[1]

    pairs[0, y] = own[0]

    def forward(ks):
        for k in ks:
            z_copy(k).wait_recv()
            for j in range(1, NY):
                f_copy(k, j).start()

    def first(block, index, slot, wide):
        lp = vec[pl.ds(pl.multiple_of(index * STEP * n, STEP * n), STEP * n), :]
        work[slot, :, 0 : wide * n] = jnp.dot(
            lp, block, preferred_element_type=F32
        ).astype(BF16)

    def second(index, slot, wide):
        lp = vec[pl.ds(pl.multiple_of(index * STEP * n, STEP * n), STEP * n), :]
        rows = []
        for p in range(wide):
            tiles = [
                work[slot, q * n : (q + 1) * n, p * n : (p + 1) * n] for q in range(STEP)
            ]
            rows.append(jnp.concatenate(tiles, axis=1))
        lhs = jnp.concatenate(rows, axis=0)
        acc[0 : wide * n, :] += jnp.dot(lhs, lp, preferred_element_type=F32)

    def group(ks, with_extra=False, beside=None):
        wide = len(ks) * NY + int(with_extra)

        def block():
            tiles = [pairs[k, yy] for k in ks for yy in range(NY)]
            if with_extra:
                tiles.append(extra[...])
            return jnp.concatenate(tiles, axis=1)

        acc[...] = jnp.zeros_like(acc)
        first(block(), 0, 0, wide)

        def step(index, _):
            slot = lax.rem(index, 2)
            if beside is not None:
                pl.when(index == steps // 2)(beside)
            first(block(), jnp.minimum(index + 1, steps - 1), 1 - slot, wide)
            second(index, slot, wide)
            return 0

        lax.fori_loop(0, steps, step, 0)

    def ready(k):
        for j in range(1, NY):
            m = k * NY + j
            source = lax.rem(y + NY - j, NY)
            copy(
                pairs.at[k, y], pairs.at[k, source], fs.at[m], fr.at[m], at(z, ahead(j))
            ).wait_recv()

    def hand(k, at_row):
        rows = acc[at_row * NY * n : (at_row + 1) * NY * n, :]
        part[k] = rows.astype(BF16).reshape(NY, n, n)
        r_copy(k).start()

    for k in range(1, NY):
        source = lax.rem(y + NY - k, NY)
        copy(own.at[0], pairs.at[0, source], hs.at[k], hr.at[k], at(z, ahead(k))).wait_recv()
    group((0,), beside=lambda: forward((1, 2, 3)))
    acc_own[...] = acc[0 : NY * n, :]
    forward((4, 5, 6, 7))

    ready(2)
    ready(3)

    @pl.when(jnp.logical_not(is_x))
    def _():
        x_copy(1).wait_recv()

    group((2, 3), with_extra=True)
    hand(2, 0)
    hand(3, 1)
    acc_x[...] = acc[2 * NY * n :, :]
    part_x[...] = acc_x[...].astype(BF16)
    on_z = z == z_x
    far_z = z != z_x
    gap_z = across(z_x)

    def rx_copy(k):
        return copy(part_x, got_zx.at[k], rxs, rxr.at[k], at(z_x, y))

    @pl.when(far_z)
    def _():
        rx_copy(gap_z).start()

    def turn(t, _):
        k = 4 + 2 * t
        ready(k)
        ready(k + 1)
        group((k, k + 1))
        hand(k, 0)
        hand(k + 1, 1)
        return 0

    lax.fori_loop(0, 2, turn, 0)

    on_x = jnp.logical_and(on_z, y == y_x)
    near_x = jnp.logical_and(on_z, y != y_x)
    gap_y = lax.rem(y_x + NY - y, NY)

    def sx_copy(k):
        return copy(send_yx, got_yx.at[k], sxs, sxr.at[k], at(z, y_x))

    @pl.when(on_z)
    def _():
        whole = acc_x[...]
        for k in range(1, NZ):
            copy(part_x, got_zx.at[k], rxs, rxr.at[k], at(across(k), y)).wait_recv()
            whole = whole + got_zx[k].astype(F32)
        acc_x[...] = whole
        send_yx[...] = whole.astype(BF16)

    @pl.when(near_x)
    def _():
        sx_copy(gap_y).start()

    ready(1)
    group((1,))
    hand(1, 0)
    total[...] = acc_own[...].reshape(NY, n, n)
    for k in (2, 3, 4, 5, 6, 7, 1):
        r_copy(k).wait_recv()
        total[...] += got_z[k].astype(F32)
    send_y[...] = total[...].astype(BF16)
    for k in range(1, NY):
        s_copy(k).start()
    out[1] = acc_x[...]

    @pl.when(on_x)
    def _():
        whole = acc_x[...]
        for k in range(1, NY):
            copy(send_yx, got_yx.at[k], sxs, sxr.at[k], at(z, ahead(k))).wait_recv()
            whole = whole + got_yx[k].astype(F32)
        out[1] = whole

    ladder = total[y]
    for k in range(1, NY):
        s_copy(k).wait_recv()
        ladder = ladder + got_y[k].astype(F32)
    out[0] = ladder

    for k in range(1, NZ):
        z_copy(k).wait_send()
        r_copy(k).wait_send()
        for j in range(1, NY):
            f_copy(k, j).wait_send()
    for k in range(1, NY):
        h_copy(k).wait_send()
        s_copy(k).wait_send()

    @pl.when(is_x)
    def _():
        def end(k, _):
            x_copy(k).wait_send()
            return 0

        lax.fori_loop(1, count, end, 0)

    @pl.when(far_z)
    def _():
        rx_copy(gap_z).wait_send()

    @pl.when(near_x)
    def _():
        sx_copy(gap_y).wait_send()


def ladder_of(vectors, own):
    n = own.shape[-1]
    dma = pltpu.SemaphoreType.DMA
    vmem = pltpu.VMEM
    wide = 2 * NY + 1
    return pl.pallas_call(
        ladder_kernel,
        out_shape=jax.ShapeDtypeStruct((2, n, n), F32),
        in_specs=[pl.BlockSpec(memory_space=vmem)] * 2,
        out_specs=pl.BlockSpec(memory_space=vmem),
        scratch_shapes=[
            vmem((NZ, NY, n, n), BF16),
            vmem((n, n), BF16),
            vmem((2, STEP * n, wide * n), BF16),
            vmem((wide * n, n), F32),
            vmem((NY * n, n), F32),
            vmem((n, n), F32),
            vmem((NZ, NY, n, n), BF16),
            vmem((n, n), BF16),
            vmem((NZ, NY, n, n), BF16),
            vmem((NZ, n, n), BF16),
            vmem((NY, n, n), F32),
            vmem((NY, n, n), BF16),
            vmem((NY, n, n), BF16),
            vmem((n, n), BF16),
            vmem((NY, n, n), BF16),
            dma((NY,)), dma((NY,)),
            dma((NZ,)), dma((NZ,)),
            dma((NY * NZ,)), dma((NY * NZ,)),
            dma((NY * NZ,)), dma,
            dma((NZ,)), dma((NZ,)),
            dma, dma((NZ,)),
            dma((NY,)), dma((NY,)),
            dma, dma((NY,)),
        ],
        compiler_params=pltpu.CompilerParams(
            collective_id=0, has_side_effects=True, vmem_limit_bytes=56 * 2**20
        ),
    )(vectors, own)


def shards(amplitudes, cholesky, other_terms):
    n = cholesky.shape[0]
    count_i = lax.axis_size("pi")
    count_j = lax.axis_size("pj")
    row = lax.axis_index("pi")
    col = lax.axis_index("pj")
    there, back = routes(count_i, count_j)
    side = col // 2
    diagonal = row == side
    second = jnp.where(row <= side, col % 2 == 1, col % 2 == 0)

    def pick(pair, which):
        return jnp.where(which, pair[1], pair[0])

    a = amplitudes[:, 0]
    o = other_terms[:, 0]
    a_kept, a_other = pick(a, second), pick(a, ~second)
    o_kept, o_other = pick(o, second), pick(o, ~second)
    axes = ("pi", "pj")
    a_in = lax.ppermute(a_other, axes, there)
    o_in = lax.ppermute(o_other, axes, there)
    mate = jnp.where(diagonal, a_kept, a_in).astype(F32)
    kept = a_kept.astype(F32) + mate.T
    extra = a_other.astype(F32) + a_in.astype(F32).T
    own = jnp.stack([kept, extra]).astype(BF16)
    vectors = jnp.transpose(cholesky, (2, 0, 1)).reshape(-1, n)
    ladder = ladder_of(vectors, own)
    o_mate = jnp.where(diagonal, o_kept, o_in)
    res_kept = o_kept + o_mate.T + 0.5 * ladder[0]
    res_extra = o_other + o_in.T + 0.5 * ladder[1]
    outgoing = jnp.where(diagonal, res_extra, res_kept)
    incoming = lax.ppermute(outgoing, axes, back).T
    keep_extra = jnp.logical_and(diagonal, col % 2 == 1)
    res_other = jnp.where(keep_extra, res_extra, incoming)
    low = jnp.where(second, res_other, res_kept)
    high = jnp.where(second, res_kept, res_other)
    return jnp.stack([low, high])[:, None]


def solution(mesh):
    return jax.shard_map(
        shards,
        mesh=mesh,
        in_specs=(P("pi", "pj", None, None), P(None, None, "pj"), P("pi", "pj", None, None)),
        out_specs=P("pi", "pj", None, None),
        check_vma=False,
    )
```

```python
import jax
import jax.numpy as jnp
from jax import lax
from jax.experimental import pallas as pl
from jax.experimental.pallas import tpu as pltpu
from jax.sharding import PartitionSpec as P

MESH = pl.DeviceIdType.MESH
NY = 4
NZ = 8
STEP = 16
F32 = jnp.float32
BF16 = jnp.bfloat16


def kept_of(row, col):
    return (col % 2) if row <= col // 2 else 1 - col % 2


def route(count_i, count_j):
    there = []
    for row in range(count_i):
        for col in range(count_j):
            other = 1 - kept_of(row, col)
            there.append((row * count_j + col, (col // 2) * count_j + 2 * row + other))
    return there


def ladder_kernel(
    vec, own, base, out,
    pairs, extra, work, acc, acc_own, acc_x, part, part_x, got_z, got_zx, total, send_y, got_y, send_yx, got_yx, done, got_m,
    hs, hr, zs, zr, fs, fr, xs, xr, rs, rr, rxs, rxr, ss, sr, sxs, sxr, ms, mr,
):
    row = lax.axis_index("pi")
    col = lax.axis_index("pj")
    y = lax.rem(col, NY)
    z = col // NY
    n = vec.shape[1]
    count = NY * NZ
    steps = n // STEP
    col_x = 2 * row + 1
    y_x = lax.rem(col_x, NY)
    z_x = col_x // NY
    side = col // 2
    kept = (col % 2 + (row - side + 15) // 16) % 2
    is_x = col == col_x
    off = row != side
    is_y = jnp.logical_and(row == side, col != col_x)

    def at(zz, yy):
        return (row, zz * NY + yy)

    def bits(v):
        return (v % 2, (v // 2) % 2, v // 4)

    def across(v):
        return sum(((a + b) % 2) * 2**k for k, (a, b) in enumerate(zip(bits(z), bits(v))))

    def ahead(k):
        return lax.rem(y + k, NY)

    def copy(src, dst, s, r, to):
        return pltpu.make_async_remote_copy(src, dst, s, r, device_id=to, device_id_type=MESH)

    barrier = pltpu.get_barrier_semaphore()

    def greet(k, _):
        pl.semaphore_signal(
            barrier, 1, device_id=(row, lax.rem(col + k, count)), device_id_type=MESH
        )
        return 0

    lax.fori_loop(1, count, greet, 0)

    @pl.when(off)
    def _():
        for k in range(2):
            pl.semaphore_signal(
                barrier, 1, device_id=(side, 2 * row + k), device_id_type=MESH
            )

    gap = row - side
    pl.semaphore_wait(barrier, count - 1 + 2 * ((gap * gap + 255) // 256))

    def h_copy(k):
        return copy(own.at[0], pairs.at[0, y], hs.at[k], hr.at[k], at(z, ahead(k)))

    def z_copy(k):
        return copy(own.at[0], pairs.at[k, y], zs.at[k], zr.at[k], at(across(k), y))

    def f_copy(k, j):
        m = k * NY + j
        return copy(pairs.at[k, y], pairs.at[k, y], fs.at[m], fr.at[m], at(z, ahead(j)))

    def x_copy(k):
        return copy(own.at[1], extra, xs.at[k], xr, (row, lax.rem(col + k, count)))

    def r_copy(k):
        return copy(part.at[k], got_z.at[k], rs.at[k], rr.at[k], at(across(k), y))

    def s_copy(k):
        return copy(send_y.at[ahead(k)], got_y.at[k], ss.at[k], sr.at[k], at(z, ahead(k)))

    for k in range(1, NY):
        h_copy(k).start()
    for k in range(1, NZ):
        z_copy(k).start()

    @pl.when(is_x)
    def _():
        def go(k, _):
            x_copy(k).start()
            return 0

        lax.fori_loop(1, count, go, 0)
        extra[...] = own[1]

    pairs[0, y] = own[0]

    def forward(ks):
        for k in ks:
            z_copy(k).wait_recv()
            for j in range(1, NY):
                f_copy(k, j).start()

    def first(block, index, slot, wide):
        lp = vec[pl.ds(pl.multiple_of(index * STEP * n, STEP * n), STEP * n), :]
        work[slot, :, 0 : wide * n] = jnp.dot(
            lp, block, preferred_element_type=F32
        ).astype(BF16)

    def second(index, slot, wide):
        lp = vec[pl.ds(pl.multiple_of(index * STEP * n, STEP * n), STEP * n), :]
        rows = []
        for p in range(wide):
            tiles = [
                work[slot, q * n : (q + 1) * n, p * n : (p + 1) * n] for q in range(STEP)
            ]
            rows.append(jnp.concatenate(tiles, axis=1))
        lhs = jnp.concatenate(rows, axis=0)
        acc[0 : wide * n, :] += jnp.dot(lhs, lp, preferred_element_type=F32)

    def group(ks, with_extra=False, beside=None):
        wide = len(ks) * NY + int(with_extra)

        def block():
            tiles = [pairs[k, yy] for k in ks for yy in range(NY)]
            if with_extra:
                tiles.append(extra[...])
            return jnp.concatenate(tiles, axis=1)

        acc[...] = jnp.zeros_like(acc)
        first(block(), 0, 0, wide)

        def step(index, _):
            slot = lax.rem(index, 2)
            if beside is not None:
                pl.when(index == steps // 2)(beside)
            first(block(), index + 1, 1 - slot, wide)
            second(index, slot, wide)
            return 0

        lax.fori_loop(0, steps - 1, step, 0)
        second(steps - 1, (steps - 1) % 2, wide)

    def ready(k):
        for j in range(1, NY):
            m = k * NY + j
            source = lax.rem(y + NY - j, NY)
            copy(
                pairs.at[k, y], pairs.at[k, source], fs.at[m], fr.at[m], at(z, ahead(j))
            ).wait_recv()

    def hand(k, at_row):
        rows = acc[at_row * NY * n : (at_row + 1) * NY * n, :]
        part[k] = rows.astype(BF16).reshape(NY, n, n)
        r_copy(k).start()

    for k in range(1, NY):
        source = lax.rem(y + NY - k, NY)
        copy(own.at[0], pairs.at[0, source], hs.at[k], hr.at[k], at(z, ahead(k))).wait_recv()
    group((0,), beside=lambda: forward((1, 2, 3)))
    acc_own[...] = acc[0 : NY * n, :]
    forward((4, 5, 6, 7))

    ready(2)
    ready(3)

    @pl.when(jnp.logical_not(is_x))
    def _():
        x_copy(1).wait_recv()

    group((2, 3), with_extra=True)
    hand(2, 0)
    hand(3, 1)
    acc_x[...] = acc[2 * NY * n :, :]
    part_x[...] = acc_x[...].astype(BF16)
    on_z = z == z_x
    far_z = z != z_x
    gap_z = across(z_x)

    def rx_copy(k):
        return copy(part_x, got_zx.at[k], rxs, rxr.at[k], at(z_x, y))

    @pl.when(far_z)
    def _():
        rx_copy(gap_z).start()

    def turn(t, _):
        k = 4 + 2 * t
        ready(k)
        ready(k + 1)
        group((k, k + 1))
        hand(k, 0)
        hand(k + 1, 1)
        return 0

    lax.fori_loop(0, 2, turn, 0)

    near_x = jnp.logical_and(on_z, y != y_x)
    gap_y = lax.rem(y_x + NY - y, NY)

    def sx_copy(k):
        return copy(send_yx, got_yx.at[k], sxs, sxr.at[k], at(z, y_x))

    @pl.when(on_z)
    def _():
        whole = acc_x[...]
        for k in range(1, NZ):
            copy(part_x, got_zx.at[k], rxs, rxr.at[k], at(across(k), y)).wait_recv()
            whole = whole + got_zx[k].astype(F32)
        acc_x[...] = whole
        send_yx[...] = whole.astype(BF16)

    @pl.when(near_x)
    def _():
        sx_copy(gap_y).start()

    ready(1)
    group((1,))
    hand(1, 0)
    total[...] = acc_own[...].reshape(NY, n, n)
    for k in (2, 3, 4, 5, 6, 7, 1):
        r_copy(k).wait_recv()
        total[...] += got_z[k].astype(F32)
    send_y[...] = total[...].astype(BF16)
    for k in range(1, NY):
        s_copy(k).start()

    def m_copy(to):
        return copy(done, got_m, ms, mr, to)

    mate = (side, 2 * row + kept)
    sibling = (row, 2 * row)

    @pl.when(is_x)
    def _():
        whole = acc_x[...]

        for k in range(1, NY):
            copy(send_yx, got_yx.at[k], sxs, sxr.at[k], at(z, ahead(k))).wait_recv()
            whole = whole + got_yx[k].astype(F32)
        done[...] = base[1] + 0.5 * whole
        m_copy(sibling).start()
        out[0] = done[...]

    ladder = total[y]
    for k in range(1, NY):
        s_copy(k).wait_recv()
        ladder = ladder + got_y[k].astype(F32)
    finished = base[0] + 0.5 * ladder
    out[kept] = finished

    @pl.when(off)
    def _():
        done[...] = finished
        m_copy(mate).start()

    for k in range(1, NZ):
        z_copy(k).wait_send()
        r_copy(k).wait_send()
        for j in range(1, NY):
            f_copy(k, j).wait_send()
    for k in range(1, NY):
        h_copy(k).wait_send()
        s_copy(k).wait_send()

    @pl.when(is_x)
    def _():
        def end(k, _):
            x_copy(k).wait_send()
            return 0

        lax.fori_loop(1, count, end, 0)

    @pl.when(far_z)
    def _():
        rx_copy(gap_z).wait_send()

    @pl.when(near_x)
    def _():
        sx_copy(gap_y).wait_send()

    @pl.when(is_x)
    def _():
        m_copy(sibling).wait_send()

    @pl.when(off)
    def _():
        m_copy(mate).wait()
        out[1 - kept] = got_m[...].T

    @pl.when(is_y)
    def _():
        m_copy((row, col_x)).wait_recv()
        out[1] = got_m[...].T


def ladder_of(vectors, own, base):
    n = own.shape[-1]
    dma = pltpu.SemaphoreType.DMA
    vmem = pltpu.VMEM
    wide = 2 * NY + 1
    return pl.pallas_call(
        ladder_kernel,
        out_shape=jax.ShapeDtypeStruct((2, n, n), F32),
        in_specs=[pl.BlockSpec(memory_space=vmem)] * 3,
        out_specs=pl.BlockSpec(memory_space=vmem),
        scratch_shapes=[
            vmem((NZ, NY, n, n), BF16),
            vmem((n, n), BF16),
            vmem((2, STEP * n, wide * n), BF16),
            vmem((wide * n, n), F32),
            vmem((NY * n, n), F32),
            vmem((n, n), F32),
            vmem((NZ, NY, n, n), BF16),
            vmem((n, n), BF16),
            vmem((NZ, NY, n, n), BF16),
            vmem((NZ, n, n), BF16),
            vmem((NY, n, n), F32),
            vmem((NY, n, n), BF16),
            vmem((NY, n, n), BF16),
            vmem((n, n), BF16),
            vmem((NY, n, n), BF16),
            vmem((n, n), F32),
            vmem((n, n), F32),
            dma((NY,)), dma((NY,)),
            dma((NZ,)), dma((NZ,)),
            dma((NY * NZ,)), dma((NY * NZ,)),
            dma((NY * NZ,)), dma,
            dma((NZ,)), dma((NZ,)),
            dma, dma((NZ,)),
            dma((NY,)), dma((NY,)),
            dma, dma((NY,)),
            dma, dma,
        ],
        compiler_params=pltpu.CompilerParams(
            collective_id=0, has_side_effects=True, vmem_limit_bytes=56 * 2**20
        ),
    )(vectors, own, base)


def shards(amplitudes, cholesky, other_terms):
    n = cholesky.shape[0]
    count_i = lax.axis_size("pi")
    count_j = lax.axis_size("pj")
    row = lax.axis_index("pi")
    col = lax.axis_index("pj")
    side = col // 2
    diagonal = row == side
    second = jnp.where(row <= side, col % 2 == 1, col % 2 == 0)

    def pick(pair, which):
        return jnp.where(which, pair[1], pair[0])

    a = amplitudes[:, 0].astype(F32)
    both = jnp.stack([a, other_terms[:, 0]], axis=1)
    kept, other = pick(both, second), pick(both, ~second)
    received = lax.ppermute(other, ("pi", "pj"), route(count_i, count_j))
    mate = jnp.where(diagonal, kept, received)
    sums = jnp.stack([kept + mate.swapaxes(1, 2), other + received.swapaxes(1, 2)])
    vectors = jnp.transpose(cholesky, (2, 0, 1)).reshape(-1, n)
    return ladder_of(vectors, sums[:, 0].astype(BF16), sums[:, 1])[:, None]


def solution(mesh):
    return jax.shard_map(
        shards,
        mesh=mesh,
        in_specs=(P("pi", "pj", None, None), P(None, None, "pj"), P("pi", "pj", None, None)),
        out_specs=P("pi", "pj", None, None),
        check_vma=False,
    )
```

```python
import jax
import jax.numpy as jnp
from jax import lax
from jax.experimental import pallas as pl
from jax.experimental.pallas import tpu as pltpu
from jax.sharding import PartitionSpec as P

MESH = pl.DeviceIdType.MESH
NY = 4
NZ = 8
STEP = 16
F32 = jnp.float32
BF16 = jnp.bfloat16


def kept_of(row, col):
    return (col % 2) if row <= col // 2 else 1 - col % 2


def route(count_i, count_j):
    there = []
    for row in range(count_i):
        for col in range(count_j):
            other = 1 - kept_of(row, col)
            there.append((row * count_j + col, (col // 2) * count_j + 2 * row + other))
    return there


def ladder_kernel(
    vec, own, others, out,
    pairs, extra, work, acc, acc_own, acc_x, part, part_x, got_z, got_zx, total, send_y, got_y, send_yx, got_yx, done, got_m, got_o, base,
    hs, hr, zs, zr, fs, fr, xs, xr, rs, rr, rxs, rxr, ss, sr, sxs, sxr, ms, mr, os, orr,
):
    row = lax.axis_index("pi")
    col = lax.axis_index("pj")
    y = lax.rem(col, NY)
    z = col // NY
    n = vec.shape[1]
    count = NY * NZ
    steps = n // STEP
    col_x = 2 * row + 1
    y_x = lax.rem(col_x, NY)
    z_x = col_x // NY
    side = col // 2
    kept = (col % 2 + (row - side + 15) // 16) % 2
    is_x = col == col_x
    off = row != side
    is_y = jnp.logical_and(row == side, col != col_x)

    def at(zz, yy):
        return (row, zz * NY + yy)

    def bits(v):
        return (v % 2, (v // 2) % 2, v // 4)

    def across(v):
        return sum(((a + b) % 2) * 2**k for k, (a, b) in enumerate(zip(bits(z), bits(v))))

    def ahead(k):
        return lax.rem(y + k, NY)

    def copy(src, dst, s, r, to):
        return pltpu.make_async_remote_copy(src, dst, s, r, device_id=to, device_id_type=MESH)

    barrier = pltpu.get_barrier_semaphore()

    def greet(k, _):
        pl.semaphore_signal(
            barrier, 1, device_id=(row, lax.rem(col + k, count)), device_id_type=MESH
        )
        return 0

    lax.fori_loop(1, count, greet, 0)

    @pl.when(off)
    def _():
        for k in range(2):
            pl.semaphore_signal(
                barrier, 1, device_id=(side, 2 * row + k), device_id_type=MESH
            )

    gap = row - side
    pl.semaphore_wait(barrier, count - 1 + 2 * ((gap * gap + 255) // 256))

    def h_copy(k):
        return copy(own.at[0], pairs.at[0, y], hs.at[k], hr.at[k], at(z, ahead(k)))

    def z_copy(k):
        return copy(own.at[0], pairs.at[k, y], zs.at[k], zr.at[k], at(across(k), y))

    def f_copy(k, j):
        m = k * NY + j
        return copy(pairs.at[k, y], pairs.at[k, y], fs.at[m], fr.at[m], at(z, ahead(j)))

    def x_copy(k):
        return copy(own.at[1], extra, xs.at[k], xr, (row, lax.rem(col + k, count)))

    def r_copy(k):
        return copy(part.at[k], got_z.at[k], rs.at[k], rr.at[k], at(across(k), y))

    def s_copy(k):
        return copy(send_y.at[ahead(k)], got_y.at[k], ss.at[k], sr.at[k], at(z, ahead(k)))

    for k in range(1, NY):
        h_copy(k).start()
    for k in range(1, NZ):
        z_copy(k).start()

    @pl.when(is_x)
    def _():
        def go(k, _):
            x_copy(k).start()
            return 0

        lax.fori_loop(1, count, go, 0)
        extra[...] = own[1]

    pairs[0, y] = own[0]

    def forward(ks):
        for k in ks:
            z_copy(k).wait_recv()
            for j in range(1, NY):
                f_copy(k, j).start()

    def first(block, index, slot, wide):
        lp = vec[pl.ds(pl.multiple_of(index * STEP * n, STEP * n), STEP * n), :]
        work[slot, :, 0 : wide * n] = jnp.dot(
            lp, block, preferred_element_type=F32
        ).astype(BF16)

    def second(index, slot, wide):
        lp = vec[pl.ds(pl.multiple_of(index * STEP * n, STEP * n), STEP * n), :]
        rows = []
        for p in range(wide):
            tiles = [
                work[slot, q * n : (q + 1) * n, p * n : (p + 1) * n] for q in range(STEP)
            ]
            rows.append(jnp.concatenate(tiles, axis=1))
        lhs = jnp.concatenate(rows, axis=0)
        acc[0 : wide * n, :] += jnp.dot(lhs, lp, preferred_element_type=F32)

    def group(ks, with_extra=False, beside=None):
        wide = len(ks) * NY + int(with_extra)

        def block():
            tiles = [pairs[k, yy] for k in ks for yy in range(NY)]
            if with_extra:
                tiles.append(extra[...])
            return jnp.concatenate(tiles, axis=1)

        acc[...] = jnp.zeros_like(acc)
        first(block(), 0, 0, wide)

        def step(index, _):
            slot = lax.rem(index, 2)
            if beside is not None:
                pl.when(index == steps // 2)(beside)
            first(block(), index + 1, 1 - slot, wide)
            second(index, slot, wide)
            return 0

        lax.fori_loop(0, steps - 1, step, 0)
        second(steps - 1, (steps - 1) % 2, wide)

    def ready(k):
        for j in range(1, NY):
            m = k * NY + j
            source = lax.rem(y + NY - j, NY)
            copy(
                pairs.at[k, y], pairs.at[k, source], fs.at[m], fr.at[m], at(z, ahead(j))
            ).wait_recv()

    def hand(k, at_row):
        rows = acc[at_row * NY * n : (at_row + 1) * NY * n, :]
        part[k] = rows.astype(BF16).reshape(NY, n, n)
        r_copy(k).start()

    for k in range(1, NY):
        source = lax.rem(y + NY - k, NY)
        copy(own.at[0], pairs.at[0, source], hs.at[k], hr.at[k], at(z, ahead(k))).wait_recv()
    group((0,), beside=lambda: forward((1, 2, 3)))
    acc_own[...] = acc[0 : NY * n, :]
    forward((4, 5, 6, 7))
    apart = (side, 2 * row + 1 - kept)
    sibling = (row, 2 * row)

    def o_copy(to):
        return copy(others.at[1], got_o, os, orr, to)

    @pl.when(off)
    def _():
        o_copy(apart).start()

    @pl.when(is_y)
    def _():
        o_copy((row, col_x)).start()

    ready(2)
    ready(3)

    @pl.when(jnp.logical_not(is_x))
    def _():
        x_copy(1).wait_recv()

    group((2, 3), with_extra=True)
    hand(2, 0)
    hand(3, 1)
    acc_x[...] = acc[2 * NY * n :, :]
    part_x[...] = acc_x[...].astype(BF16)
    on_z = z == z_x
    far_z = z != z_x
    gap_z = across(z_x)

    def rx_copy(k):
        return copy(part_x, got_zx.at[k], rxs, rxr.at[k], at(z_x, y))

    @pl.when(far_z)
    def _():
        rx_copy(gap_z).start()

    def turn(t, _):
        k = 4 + 2 * t
        ready(k)
        ready(k + 1)
        group((k, k + 1))
        hand(k, 0)
        hand(k + 1, 1)
        return 0

    lax.fori_loop(0, 2, turn, 0)

    near_x = jnp.logical_and(on_z, y != y_x)
    gap_y = lax.rem(y_x + NY - y, NY)

    def sx_copy(k):
        return copy(send_yx, got_yx.at[k], sxs, sxr.at[k], at(z, y_x))

    @pl.when(on_z)
    def _():
        whole = acc_x[...]
        for k in range(1, NZ):
            copy(part_x, got_zx.at[k], rxs, rxr.at[k], at(across(k), y)).wait_recv()
            whole = whole + got_zx[k].astype(F32)
        acc_x[...] = whole
        send_yx[...] = whole.astype(BF16)

    @pl.when(near_x)
    def _():
        sx_copy(gap_y).start()

    @pl.when(off)
    def _():
        o_copy(apart).wait_recv()
        base[...] = others[0] + got_o[...].T

    @pl.when(jnp.logical_not(off))
    def _():
        base[...] = others[0] + others[0].T

    @pl.when(is_x)
    def _():
        o_copy(sibling).wait_recv()
        done[...] = others[1] + got_o[...].T

    ready(1)
    group((1,))
    hand(1, 0)
    total[...] = acc_own[...].reshape(NY, n, n)
    for k in (2, 3, 4, 5, 6, 7, 1):
        r_copy(k).wait_recv()
        total[...] += got_z[k].astype(F32)
    send_y[...] = total[...].astype(BF16)
    for k in range(1, NY):
        s_copy(k).start()

    def m_copy(to):
        return copy(done, got_m, ms, mr, to)

    mate = (side, 2 * row + kept)

    @pl.when(is_x)
    def _():
        whole = acc_x[...]

        for k in range(1, NY):
            copy(send_yx, got_yx.at[k], sxs, sxr.at[k], at(z, ahead(k))).wait_recv()
            whole = whole + got_yx[k].astype(F32)
        done[...] += 0.5 * whole
        m_copy(sibling).start()
        out[0] = done[...]

    ladder = total[y]
    for k in range(1, NY):
        s_copy(k).wait_recv()
        ladder = ladder + got_y[k].astype(F32)
    finished = base[...] + 0.5 * ladder
    out[kept] = finished

    @pl.when(off)
    def _():
        done[...] = finished
        m_copy(mate).start()

    for k in range(1, NZ):
        z_copy(k).wait_send()
        r_copy(k).wait_send()
        for j in range(1, NY):
            f_copy(k, j).wait_send()
    for k in range(1, NY):
        h_copy(k).wait_send()
        s_copy(k).wait_send()

    @pl.when(is_x)
    def _():
        def end(k, _):
            x_copy(k).wait_send()
            return 0

        lax.fori_loop(1, count, end, 0)

    @pl.when(far_z)
    def _():
        rx_copy(gap_z).wait_send()

    @pl.when(near_x)
    def _():
        sx_copy(gap_y).wait_send()

    @pl.when(off)
    def _():
        o_copy(apart).wait_send()

    @pl.when(is_y)
    def _():
        o_copy((row, col_x)).wait_send()

    @pl.when(is_x)
    def _():
        m_copy(sibling).wait_send()

    @pl.when(off)
    def _():
        m_copy(mate).wait()
        out[1 - kept] = got_m[...].T

    @pl.when(is_y)
    def _():
        m_copy((row, col_x)).wait_recv()
        out[1] = got_m[...].T


def ladder_of(vectors, own, others):
    n = own.shape[-1]
    dma = pltpu.SemaphoreType.DMA
    vmem = pltpu.VMEM
    wide = 2 * NY + 1
    return pl.pallas_call(
        ladder_kernel,
        out_shape=jax.ShapeDtypeStruct((2, n, n), F32),
        in_specs=[pl.BlockSpec(memory_space=vmem)] * 3,
        out_specs=pl.BlockSpec(memory_space=vmem),
        scratch_shapes=[
            vmem((NZ, NY, n, n), BF16),
            vmem((n, n), BF16),
            vmem((2, STEP * n, wide * n), BF16),
            vmem((wide * n, n), F32),
            vmem((NY * n, n), F32),
            vmem((n, n), F32),
            vmem((NZ, NY, n, n), BF16),
            vmem((n, n), BF16),
            vmem((NZ, NY, n, n), BF16),
            vmem((NZ, n, n), BF16),
            vmem((NY, n, n), F32),
            vmem((NY, n, n), BF16),
            vmem((NY, n, n), BF16),
            vmem((n, n), BF16),
            vmem((NY, n, n), BF16),
            vmem((n, n), F32),
            vmem((n, n), F32),
            vmem((n, n), F32),
            vmem((n, n), F32),
            dma((NY,)), dma((NY,)),
            dma((NZ,)), dma((NZ,)),
            dma((NY * NZ,)), dma((NY * NZ,)),
            dma((NY * NZ,)), dma,
            dma((NZ,)), dma((NZ,)),
            dma, dma((NZ,)),
            dma((NY,)), dma((NY,)),
            dma, dma((NY,)),
            dma, dma,
            dma, dma,
        ],
        compiler_params=pltpu.CompilerParams(
            collective_id=0, has_side_effects=True, vmem_limit_bytes=56 * 2**20
        ),
    )(vectors, own, others)


def shards(amplitudes, cholesky, other_terms):
    n = cholesky.shape[0]
    count_i = lax.axis_size("pi")
    count_j = lax.axis_size("pj")
    row = lax.axis_index("pi")
    col = lax.axis_index("pj")
    side = col // 2
    diagonal = row == side
    second = jnp.where(row <= side, col % 2 == 1, col % 2 == 0)

    def pick(pair, which):
        return jnp.where(which, pair[1], pair[0])

    a = amplitudes[:, 0]
    o = other_terms[:, 0]
    kept, other = pick(a, second), pick(a, ~second)
    received = lax.ppermute(other, ("pi", "pj"), route(count_i, count_j))
    mate = jnp.where(diagonal, kept, received)
    own = jnp.stack(
        [
            kept.astype(F32) + mate.astype(F32).T,
            other.astype(F32) + received.astype(F32).T,
        ]
    ).astype(BF16)
    others = jnp.stack([pick(o, second), pick(o, ~second)])
    vectors = jnp.transpose(cholesky, (2, 0, 1)).reshape(-1, n)
    return ladder_of(vectors, own, others)[:, None]


def solution(mesh):
    return jax.shard_map(
        shards,
        mesh=mesh,
        in_specs=(P("pi", "pj", None, None), P(None, None, "pj"), P("pi", "pj", None, None)),
        out_specs=P("pi", "pj", None, None),
        check_vma=False,
    )
```
